32 devices in a mesh: groups: 2 (over x), slab: 16 (over z, y, core).
Axes of the slice: x: 2, y: 2, z: 4, core: 2. Of those that a mesh axis runs over, the one named last changes fastest.
Arguments:
- volume: float32 [64, 16, 16], P(('groups', 'slab')), parts along dimension 0, may hold values from -6 to 6
- conv_first: float32 [16, 9], replicated, may hold values from -2 to 2
- first_bias: float32 [16], replicated, may hold values from -1.75 to 1.75
- conv_second: float32 [9, 16, 16], replicated, may hold values from -0.5 to 0.5
- second_bias: float32 [16], replicated, may hold values from -1.75 to 1.75
- head_weight: float32 [4, 16], replicated, may hold values from -1.5 to 1.5
- head_bias: float32 [4], replicated, may hold values from -3 to 3
- merging: float32 [3, 4], replicated, may hold values from 0.2 to 1
Outputs:
- cleaned: float32 [4, 64, 16, 16], P(None, ('groups', 'slab')), parts along dimension 1
The draws below stay inside these ranges and needn't reach their ends.
There are 2 independent parts, one for each index of `groups`. The reference program is written for one: setup_inputs(seed, part) draws one part's arguments, and reference() takes and returns one part's arrays. A program takes and returns all parts, laid end to end along the dimension named above; an argument that names none is the same for every part. Nothing has to cross between parts.
All inputs are finite; a program needn't handle non-finite values.
Results may differ from the reference program's by a relative error of at most 0.0001.
Values sent between devices are 32-bit elements; how exact they have to be, the bound alone decides.
A program may use at most 64 MiB of HBM per device.

```python
import jax
import jax.numpy as jnp
from jax import lax

CXY = 1
CZ = 2
CH = 16
HEADS = 4
NX = 16
NY = 16
NZ = 32


def levels(stream_key, extent, cuts, smallest, largest):
    def one(axis_at, parts):
        draws = jax.random.uniform(jax.random.fold_in(jax.random.fold_in(stream_key, 6), axis_at), (parts,), jnp.float32, smallest / len(cuts), largest / len(cuts))
        return jnp.repeat(jnp.exp(draws), extent[axis_at] // parts).reshape((-1,) + (1,) * (len(extent) - axis_at - 1))

    factor_of = one(*cuts[0])
    for cut in cuts[1:]:
        factor_of = factor_of * one(*cut)
    return factor_of


def noise(rng, shape, width, limit, cuts=(), kind=jnp.bfloat16):
    gain = levels(rng, shape, cuts, -0.22, 0.18) if cuts else 1.0
    entries = jax.random.normal(rng, shape, jnp.float32) * width * gain
    return jnp.minimum(jnp.maximum(entries, -limit), limit).astype(kind)


def setup_inputs(seed: int = 0, part: int = 0) -> dict:
    key_of = jax.random.split(jax.random.key(seed), 9)
    part_keys = jax.random.split(jax.random.fold_in(key_of[8], part), 9)
    volume = noise(part_keys[0], (NZ, NX, NY), 1.0, 6.0, ((0, 16),), jnp.float32)
    conv_first = noise(key_of[1], (CH, 9), 9 ** -0.5, 2.0, (), jnp.float32)
    first_bias = noise(key_of[2], (CH,), 0.3, 1.75, (), jnp.float32)
    conv_second = noise(key_of[3], (9, CH, CH), (9 * CH) ** -0.5, 0.5, (), jnp.float32)
    second_bias = noise(key_of[4], (CH,), 0.3, 1.75, (), jnp.float32)
    head_weight = noise(key_of[5], (HEADS, CH), CH ** -0.5, 1.5, (), jnp.float32)
    head_bias = noise(key_of[6], (HEADS,), 0.5, 3.0, (), jnp.float32)
    merging = jnp.clip(jax.random.uniform(key_of[7], (3, HEADS), jnp.float32, 0.2, 1.0), 0.2, 1.0)
    return {"volume": volume, "conv_first": conv_first, "first_bias": first_bias, "conv_second": conv_second, "second_bias": second_bias, "head_weight": head_weight, "head_bias": head_bias, "merging": merging}


exact_prec = lax.Precision.HIGHEST


def plane_features(planes, conv_first, first_bias, conv_second, second_bias):
    rows_in = planes.shape[1]
    cols_in = planes.shape[2]
    padded = jnp.pad(planes, ((0, 0), (1, 1), (1, 1)))
    tap_stack = jnp.stack([padded[:, row_off:row_off + rows_in, col_off:col_off + cols_in] for row_off in range(3) for col_off in range(3)])
    hidden_one = jnp.einsum("ct,tbhw->cbhw", conv_first, tap_stack, precision=exact_prec) + first_bias[:, None, None, None]
    hidden_one = jnp.maximum(hidden_one, 0.0)
    padded_one = jnp.pad(hidden_one, ((0, 0), (0, 0), (1, 1), (1, 1)))
    summed = jnp.zeros(hidden_one.shape, jnp.float32) + second_bias[:, None, None, None]
    for row_off in range(3):
        for col_off in range(3):
            window = padded_one[:, :, row_off:row_off + rows_in, col_off:col_off + cols_in]
            summed = summed + jnp.einsum("oi,ibhw->obhw", conv_second[3 * row_off + col_off], window, precision=exact_prec)
    return jnp.maximum(summed, 0.0)


def apply_heads(features, head_weight, head_bias):
    return jnp.einsum("ko,obhw->kbhw", head_weight, features, precision=exact_prec) + head_bias[:, None, None, None]


def median_three(lower_side, middle, upper_side):
    return jnp.maximum(jnp.minimum(lower_side, middle), jnp.minimum(jnp.maximum(lower_side, middle), upper_side))


def predict_planes(source, block_len, conv_first, first_bias, conv_second, second_bias, head_weight, head_bias):
    block_count = source.shape[0] // block_len
    blocks = source.reshape(block_count, block_len, source.shape[1], source.shape[2])

    def one_block(planes):
        return apply_heads(plane_features(planes, conv_first, first_bias, conv_second, second_bias), head_weight, head_bias)

    result = lax.map(one_block, blocks)
    result = jnp.transpose(result, (1, 0, 2, 3, 4))
    return result.reshape(result.shape[0], source.shape[0], source.shape[1], source.shape[2])


def reference(volume, conv_first, first_bias, conv_second, second_bias, head_weight, head_bias, merging):
    xy_pred = predict_planes(volume, CZ, conv_first, first_bias, conv_second, second_bias, head_weight, head_bias)
    xz_pred = predict_planes(jnp.transpose(volume, (2, 0, 1)), CXY, conv_first, first_bias, conv_second, second_bias, head_weight, head_bias)
    xz_pred = jnp.transpose(xz_pred, (0, 2, 3, 1))
    yz_pred = predict_planes(jnp.transpose(volume, (1, 0, 2)), CXY, conv_first, first_bias, conv_second, second_bias, head_weight, head_bias)
    yz_pred = jnp.transpose(yz_pred, (0, 2, 1, 3))
    merged_pred = merging[0][:, None, None, None] * xy_pred + merging[1][:, None, None, None] * xz_pred + merging[2][:, None, None, None] * yz_pred
    lower_side = jnp.concatenate([merged_pred[:, :1], merged_pred[:, :-1]], axis=1)
    upper_side = jnp.concatenate([merged_pred[:, 1:], merged_pred[:, -1:]], axis=1)
    return median_three(lower_side, merged_pred, upper_side)
```

```python
import jax
import jax.numpy as jnp
from jax import lax
from jax.experimental import pallas as pl
from jax.experimental.pallas import tpu as pltpu
from jax.sharding import PartitionSpec as P

exact_prec = lax.Precision.HIGHEST


def with_halo(block, sides, width):
    for axis, dim in sides:
        count = lax.axis_size(axis)
        forward = [(i, i + 1) for i in range(count - 1)]
        backward = [(target, source) for source, target in forward]
        low = lax.ppermute(
            lax.slice_in_dim(block, block.shape[dim] - width, None, axis=dim), axis, forward
        )
        high = lax.ppermute(lax.slice_in_dim(block, 0, width, axis=dim), axis, backward)
        block = jnp.concatenate([low, block, high], axis=dim)
    return block


def plane_features(planes, conv_first, first_bias, conv_second, second_bias):
    rows_in = planes.shape[1]
    cols_in = planes.shape[2]
    padded = jnp.pad(planes, ((0, 0), (1, 1), (1, 1)))
    tap_stack = jnp.stack(
        [
            padded[:, row_off : row_off + rows_in, col_off : col_off + cols_in]
            for row_off in range(3)
            for col_off in range(3)
        ]
    )
    hidden_one = (
        jnp.einsum("ct,tbhw->cbhw", conv_first, tap_stack, precision=exact_prec)
        + first_bias[:, None, None, None]
    )
    hidden_one = jnp.maximum(hidden_one, 0.0)
    padded_one = jnp.pad(hidden_one, ((0, 0), (0, 0), (1, 1), (1, 1)))
    summed = jnp.zeros(hidden_one.shape, jnp.float32) + second_bias[:, None, None, None]
    for row_off in range(3):
        for col_off in range(3):
            window = padded_one[:, :, row_off : row_off + rows_in, col_off : col_off + cols_in]
            summed = summed + jnp.einsum(
                "oi,ibhw->obhw", conv_second[3 * row_off + col_off], window, precision=exact_prec
            )
    return jnp.maximum(summed, 0.0)


def apply_heads(features, head_weight, head_bias):
    return (
        jnp.einsum("ko,obhw->kbhw", head_weight, features, precision=exact_prec)
        + head_bias[:, None, None, None]
    )


def median_three(lower_side, middle, upper_side):
    return jnp.maximum(
        jnp.minimum(lower_side, middle), jnp.minimum(jnp.maximum(lower_side, middle), upper_side)
    )


def predict_each(planes, conv_first, first_bias, conv_second, second_bias, head_weight, head_bias):

    def one_plane(single):
        features = plane_features(single[None], conv_first, first_bias, conv_second, second_bias)
        return apply_heads(features, head_weight, head_bias)[:, 0]

    result = lax.map(one_plane, planes)
    return jnp.transpose(result, (1, 0, 2, 3))


def on_device(
    volume, conv_first, first_bias, conv_second, second_bias, head_weight, head_bias, merging
):
    slab_count = lax.axis_size("slab")
    position = lax.axis_index("slab")
    across_y, across_x = (
        lax.all_to_all(
            jnp.transpose(volume, (2, 0, 1)), "slab", split_axis=0, concat_axis=1, tiled=True
        ),
        lax.all_to_all(
            jnp.transpose(volume, (1, 0, 2)), "slab", split_axis=0, concat_axis=1, tiled=True
        ),
    )
    xy_pred = predict_each(
        volume, conv_first, first_bias, conv_second, second_bias, head_weight, head_bias
    )
    xz_load = predict_each(
        across_y, conv_first, first_bias, conv_second, second_bias, head_weight, head_bias
    )
    yz_load = predict_each(
        across_x, conv_first, first_bias, conv_second, second_bias, head_weight, head_bias
    )
    xz_back = lax.all_to_all(xz_load, "slab", split_axis=2, concat_axis=1, tiled=True)
    yz_back = lax.all_to_all(yz_load, "slab", split_axis=2, concat_axis=1, tiled=True)
    xz_pred = jnp.transpose(xz_back, (0, 2, 3, 1))
    yz_pred = jnp.transpose(yz_back, (0, 2, 1, 3))
    merged_pred = (
        merging[0][:, None, None, None] * xy_pred
        + merging[1][:, None, None, None] * xz_pred
        + merging[2][:, None, None, None] * yz_pred
    )
    padded = with_halo(merged_pred, (("slab", 1),), 1)
    under_rim = jnp.where(position == 0, merged_pred[:, :1], padded[:, :1])
    over_rim = jnp.where(position == slab_count - 1, merged_pred[:, -1:], padded[:, -1:])
    lower_side = jnp.concatenate([under_rim, merged_pred[:, :-1]], axis=1)
    upper_side = jnp.concatenate([merged_pred[:, 1:], over_rim], axis=1)
    return median_three(lower_side, merged_pred, upper_side)


MESH = pl.DeviceIdType.MESH
f32 = jnp.float32
bf16 = jnp.bfloat16
REACH = 3


def split(x):
    hi = x.astype(bf16)
    return hi, (x - hi.astype(f32)).astype(bf16)


def mm(a, b):
    return lax.dot_general(a, b, (((1,), (0,)), ((), ())), preferred_element_type=f32)


def mm_nt(a, b):
    return lax.dot_general(a, b, (((1,), (1,)), ((), ())), preferred_element_type=f32)


def exact_mm(a, b):
    return lax.dot_general(
        a, b, (((1,), (0,)), ((), ())), preferred_element_type=f32, precision=exact_prec
    )


def product(mul, a, b):
    (a_hi, a_lo), (b_hi, b_lo) = a, b
    return mul(a_hi, b_hi) + (mul(a_hi, b_lo) + mul(a_lo, b_hi))


def iota(shape, dim):
    return lax.broadcasted_iota(jnp.int32, shape, dim)


def halo_plan(cz):
    plan = []
    left = REACH
    distance = 1
    while left > 0:
        count = min(cz, left)
        plan.append((distance, count))
        left -= count
        distance += 1
    return plan


def brick_kernel(
    slabs,
    vol_ref,
    w1_ref,
    b1_ref,
    w2_ref,
    b2_ref,
    hw_ref,
    hb_ref,
    mg_ref,
    out_ref,
    vbuf,
    pad_ref,
    send_sem,
    recv_sem,
):
    cz, nx, ny = vol_ref.shape
    ch = w1_ref.shape[0]
    heads = hw_ref.shape[0]
    lanes = ny * ch
    zi, zf, zo = cz + 6, cz + 4, cz + 2
    pos = lax.axis_index("slab")
    plan = halo_plan(cz)

    vbuf[...] = jnp.zeros(vbuf.shape, f32)
    vbuf[REACH : REACH + cz] = vol_ref[...]

    sends = []
    for distance, count in plan:
        sends.append((distance, cz - count, count, REACH - (distance - 1) * cz - count))
        sends.append((-distance, 0, count, REACH + distance * cz))

    def inside(index):
        return jnp.logical_and(index >= 0, index < slabs)

    barrier = pltpu.get_barrier_semaphore()
    expected = jnp.int32(0)
    for offset, _, _, _ in sends:
        there = inside(pos + offset)
        expected = expected + there.astype(jnp.int32)

        @pl.when(there)
        def _():
            pl.semaphore_signal(
                barrier, inc=1, device_id={"slab": pos + offset}, device_id_type=MESH
            )

    pl.semaphore_wait(barrier, expected)

    def copy_of(at):
        offset, first, count, slot = sends[at]
        return pltpu.make_async_remote_copy(
            src_ref=vol_ref.at[pl.ds(first, count)],
            dst_ref=vbuf.at[pl.ds(slot, count)],
            send_sem=send_sem.at[at],
            recv_sem=recv_sem.at[at],
            device_id={"slab": pos + offset},
            device_id_type=MESH,
        )

    for at, (offset, _, _, _) in enumerate(sends):

        @pl.when(inside(pos + offset))
        def _():
            copy_of(at).start()

    spread = (jnp.bitwise_and(iota((ch, lanes), 1), ch - 1) == iota((ch, lanes), 0)).astype(f32)
    b1 = exact_mm(b1_ref[...].reshape(1, ch), spread)
    b2 = exact_mm(b2_ref[...].reshape(1, ch), spread)
    w1_rows = exact_mm(w1_ref[...].T, spread)
    out_col = iota((ch, lanes), 1) // ch
    in_col = iota((ny, lanes), 0)
    col_gap = in_col - iota((ny, lanes), 1) // ch + 1
    first_parts = []
    for a in range(3):
        part = jnp.zeros((ny, lanes), f32)
        for b in range(3):
            row = w1_rows[3 * a + b : 3 * a + b + 1]
            part = jnp.where(col_gap == b, row, part)
        first_parts.append(part)
    first_w = split(jnp.concatenate(first_parts, axis=0))

    w2_t = w2_ref[...].reshape(9 * ch, ch).T
    spread_b = spread.astype(bf16)
    second_w = []
    for a in range(3):
        tiles = []
        for b in range(3):
            tap = 3 * a + b
            tiles.append([mm(v, spread_b) for v in split(w2_t[:, tap * ch : (tap + 1) * ch])])
        halves = []
        for half in range(2):
            rows = []
            for col in range(ny):
                block = jnp.where(out_col == col + 1, tiles[0][half], 0.0)
                block = jnp.where(out_col == col, tiles[1][half], block)
                block = jnp.where(out_col == col - 1, tiles[2][half], block)
                rows.append(block)
            halves.append(jnp.concatenate(rows, axis=0).astype(bf16))
        second_w.append(tuple(halves))

    hw_rows = exact_mm(hw_ref[...], spread)
    same = iota((ny, lanes), 0) == iota((ny, lanes), 1) // ch
    head_w = split(
        jnp.concatenate(
            [jnp.where(same, hw_rows[k : k + 1], 0.0) for k in range(heads)], axis=0
        )
    )

    for at, (offset, _, _, _) in enumerate(sends):

        @pl.when(inside(pos - offset))
        def _():
            copy_of(at).wait_recv()

    vol = vbuf[...].reshape(zi * nx, ny)
    vol_t = vol.T
    taps_yz = jnp.concatenate([vol[a * nx : (a + zf) * nx] for a in range(3)], axis=1)
    taps_xz = jnp.concatenate([vol_t[:, j * nx : (j + 3) * nx] for j in range(zf)], axis=0)
    row_x = jnp.bitwise_and(iota((zo * nx, ny), 0), nx - 1)
    mid = vol[2 * nx : (2 + zo) * nx]
    above = jnp.where(row_x == 0, 0.0, vol[2 * nx - 1 : (2 + zo) * nx - 1])
    below = jnp.where(row_x == nx - 1, 0.0, vol[2 * nx + 1 : (2 + zo) * nx + 1])
    taps_xy = jnp.concatenate([above, mid, below], axis=1)
    taps = split(jnp.concatenate([taps_xy, taps_xz, taps_yz], axis=0))
    hidden = jnp.maximum(product(mm, taps, first_w) + b1, 0.0)

    at_xz, at_yz, at_end = zo * nx, zo * nx + zf * ny, zo * nx + zf * ny + zf * nx
    slice_of = iota((zf * nx, lanes), 0) // nx + (pos * cz - 2)
    valid = jnp.logical_and(slice_of >= 0, slice_of < slabs * cz)
    hid_xz = split(jnp.where(valid, hidden[at_xz:at_yz], 0.0))
    hid_yz = split(jnp.where(valid, hidden[at_yz:at_end], 0.0))

    pad_ref[:, 0:8] = jnp.zeros((zo, 8, lanes), f32)
    pad_ref[:, nx + 8 : nx + 16] = jnp.zeros((zo, 8, lanes), f32)
    pad_ref[:, 8 : nx + 8] = hidden[:at_xz].reshape(zo, nx, lanes)

    summed = b2
    for a in range(3):
        hid_xy = split(pad_ref[:, 7 + a : 7 + a + nx].reshape(zo * nx, lanes))
        rows = tuple(
            jnp.concatenate(
                [
                    hid_xy[half],
                    hid_xz[half][a * ny : (a + zo) * ny],
                    hid_yz[half][a * nx : (a + zo) * nx],
                ],
                axis=0,
            )
            for half in range(2)
        )
        summed = summed + product(mm, rows, second_w[a])
    feats = split(jnp.maximum(summed, 0.0))
    f_xy, f_xz, f_yz = (
        tuple(v[j * zo * nx : (j + 1) * zo * nx] for v in feats) for j in range(3)
    )

    p_xy = product(mm_nt, f_xy, head_w)
    p_yz = product(mm_nt, f_yz, head_w)
    p_xz = product(mm_nt, head_w, f_xz)
    for k in range(heads):
        bias = hb_ref[k]
        w_xy, w_xz, w_yz = mg_ref[0, k], mg_ref[1, k], mg_ref[2, k]
        cols = slice(k * ny, (k + 1) * ny)
        merged = []
        flat = w_xy * (p_xy[:, cols] + bias) + w_yz * (p_yz[:, cols] + bias)
        side = w_xz * (p_xz[cols] + bias)
        for z in range(zo):
            merged.append(flat[z * nx : (z + 1) * nx] + side[:, z * ny : (z + 1) * ny])
        merged[0] = jnp.where(pos == 0, merged[1], merged[0])
        merged[-1] = jnp.where(pos == slabs - 1, merged[-2], merged[-1])
        for z in range(cz):
            out_ref[k, z] = median_three(merged[z], merged[z + 1], merged[z + 2])

    for at, (offset, _, _, _) in enumerate(sends):

        @pl.when(inside(pos + offset))
        def _():
            copy_of(at).wait_send()


def on_device_small(volume, *params):
    cz, nx, ny = volume.shape
    ch = params[0].shape[0]
    heads = params[4].shape[0]
    slabs = lax.axis_size("slab")
    copies = 2 * len(halo_plan(cz))
    vmem = pl.BlockSpec(memory_space=pltpu.VMEM)
    smem = pl.BlockSpec(memory_space=pltpu.SMEM)
    return pl.pallas_call(
        lambda *refs: brick_kernel(slabs, *refs),
        out_shape=jax.ShapeDtypeStruct((heads, cz, nx, ny), f32),
        in_specs=[vmem] * 6 + [smem] * 2,
        out_specs=vmem,
        scratch_shapes=[
            pltpu.VMEM((cz + 2 * REACH, nx, ny), f32),
            pltpu.VMEM((cz + 2, nx + 16, ny * ch), f32),
            pltpu.SemaphoreType.DMA((copies,)),
            pltpu.SemaphoreType.DMA((copies,)),
        ],
        compiler_params=pltpu.CompilerParams(
            collective_id=0, has_side_effects=True, vmem_limit_bytes=32 * 1024 * 1024
        ),
        name="brick",
    )(volume, *params)


def on_device_any(volume, *params):
    _, nx, ny = volume.shape
    ch = params[0].shape[0]
    if nx == ny and nx % 16 == 0 and ch % 16 == 0 and nx & (nx - 1) == 0 and ch & (ch - 1) == 0:
        if ny * ch <= 512:
            return on_device_small(volume, *params)
    return on_device(volume, *params)


def solution(mesh):
    in_specs = (P(("groups", "slab"), None, None), P(), P(), P(), P(), P(), P(), P())
    out_specs = P(None, ("groups", "slab"), None, None)
    return jax.shard_map(
        on_device_any, mesh=mesh, in_specs=in_specs, out_specs=out_specs, check_vma=False
    )
```

```python
import jax
import jax.numpy as jnp
from jax import lax
from jax.experimental import pallas as pl
from jax.experimental.pallas import tpu as pltpu
from jax.sharding import PartitionSpec as P

exact_prec = lax.Precision.HIGHEST


def with_halo(block, sides, width):
    for axis, dim in sides:
        count = lax.axis_size(axis)
        forward = [(i, i + 1) for i in range(count - 1)]
        backward = [(target, source) for source, target in forward]
        low = lax.ppermute(
            lax.slice_in_dim(block, block.shape[dim] - width, None, axis=dim), axis, forward
        )
        high = lax.ppermute(lax.slice_in_dim(block, 0, width, axis=dim), axis, backward)
        block = jnp.concatenate([low, block, high], axis=dim)
    return block


def plane_features(planes, conv_first, first_bias, conv_second, second_bias):
    rows_in = planes.shape[1]
    cols_in = planes.shape[2]
    padded = jnp.pad(planes, ((0, 0), (1, 1), (1, 1)))
    tap_stack = jnp.stack(
        [
            padded[:, row_off : row_off + rows_in, col_off : col_off + cols_in]
            for row_off in range(3)
            for col_off in range(3)
        ]
    )
    hidden_one = (
        jnp.einsum("ct,tbhw->cbhw", conv_first, tap_stack, precision=exact_prec)
        + first_bias[:, None, None, None]
    )
    hidden_one = jnp.maximum(hidden_one, 0.0)
    padded_one = jnp.pad(hidden_one, ((0, 0), (0, 0), (1, 1), (1, 1)))
    summed = jnp.zeros(hidden_one.shape, jnp.float32) + second_bias[:, None, None, None]
    for row_off in range(3):
        for col_off in range(3):
            window = padded_one[:, :, row_off : row_off + rows_in, col_off : col_off + cols_in]
            summed = summed + jnp.einsum(
                "oi,ibhw->obhw", conv_second[3 * row_off + col_off], window, precision=exact_prec
            )
    return jnp.maximum(summed, 0.0)


def apply_heads(features, head_weight, head_bias):
    return (
        jnp.einsum("ko,obhw->kbhw", head_weight, features, precision=exact_prec)
        + head_bias[:, None, None, None]
    )


def median_three(lower_side, middle, upper_side):
    return jnp.maximum(
        jnp.minimum(lower_side, middle), jnp.minimum(jnp.maximum(lower_side, middle), upper_side)
    )


def predict_each(planes, conv_first, first_bias, conv_second, second_bias, head_weight, head_bias):

    def one_plane(single):
        features = plane_features(single[None], conv_first, first_bias, conv_second, second_bias)
        return apply_heads(features, head_weight, head_bias)[:, 0]

    result = lax.map(one_plane, planes)
    return jnp.transpose(result, (1, 0, 2, 3))


def on_device(
    volume, conv_first, first_bias, conv_second, second_bias, head_weight, head_bias, merging
):
    slab_count = lax.axis_size("slab")
    position = lax.axis_index("slab")
    across_y, across_x = (
        lax.all_to_all(
            jnp.transpose(volume, (2, 0, 1)), "slab", split_axis=0, concat_axis=1, tiled=True
        ),
        lax.all_to_all(
            jnp.transpose(volume, (1, 0, 2)), "slab", split_axis=0, concat_axis=1, tiled=True
        ),
    )
    xy_pred = predict_each(
        volume, conv_first, first_bias, conv_second, second_bias, head_weight, head_bias
    )
    xz_load = predict_each(
        across_y, conv_first, first_bias, conv_second, second_bias, head_weight, head_bias
    )
    yz_load = predict_each(
        across_x, conv_first, first_bias, conv_second, second_bias, head_weight, head_bias
    )
    xz_back = lax.all_to_all(xz_load, "slab", split_axis=2, concat_axis=1, tiled=True)
    yz_back = lax.all_to_all(yz_load, "slab", split_axis=2, concat_axis=1, tiled=True)
    xz_pred = jnp.transpose(xz_back, (0, 2, 3, 1))
    yz_pred = jnp.transpose(yz_back, (0, 2, 1, 3))
    merged_pred = (
        merging[0][:, None, None, None] * xy_pred
        + merging[1][:, None, None, None] * xz_pred
        + merging[2][:, None, None, None] * yz_pred
    )
    padded = with_halo(merged_pred, (("slab", 1),), 1)
    under_rim = jnp.where(position == 0, merged_pred[:, :1], padded[:, :1])
    over_rim = jnp.where(position == slab_count - 1, merged_pred[:, -1:], padded[:, -1:])
    lower_side = jnp.concatenate([under_rim, merged_pred[:, :-1]], axis=1)
    upper_side = jnp.concatenate([merged_pred[:, 1:], over_rim], axis=1)
    return median_three(lower_side, merged_pred, upper_side)


MESH = pl.DeviceIdType.MESH
f32 = jnp.float32
bf16 = jnp.bfloat16
REACH = 3


def split(x):
    hi = x.astype(bf16)
    return hi, (x - hi.astype(f32)).astype(bf16)


def mm(a, b):
    return lax.dot_general(a, b, (((1,), (0,)), ((), ())), preferred_element_type=f32)


def mm_nt(a, b):
    return lax.dot_general(a, b, (((1,), (1,)), ((), ())), preferred_element_type=f32)


def exact_mm(a, b):
    return lax.dot_general(
        a, b, (((1,), (0,)), ((), ())), preferred_element_type=f32, precision=exact_prec
    )


def product(mul, a, b):
    (a_hi, a_lo), (b_hi, b_lo) = a, b
    return mul(a_hi, b_hi) + (mul(a_hi, b_lo) + mul(a_lo, b_hi))


def iota(shape, dim):
    return lax.broadcasted_iota(jnp.int32, shape, dim)


def halo_plan(cz):
    plan = []
    left = REACH
    distance = 1
    while left > 0:
        count = min(cz, left)
        plan.append((distance, count))
        left -= count
        distance += 1
    return plan


def brick_kernel(
    slabs,
    vol_hbm,
    w1_hbm,
    b1_hbm,
    w2_hbm,
    b2_hbm,
    hw_hbm,
    hb_hbm,
    mg_hbm,
    out_ref,
    vbuf,
    w1_ref,
    b1_ref,
    w2_ref,
    b2_ref,
    hw_ref,
    hb_ref,
    mg_ref,
    pad_ref,
    send_sem,
    recv_sem,
    load_sem,
):
    cz, nx, ny = vol_hbm.shape
    ch = w1_ref.shape[0]
    heads = hw_ref.shape[0]
    lanes = ny * ch
    zi, zf, zo = cz + 6, cz + 4, cz + 2
    pos = lax.axis_index("slab")
    plan = halo_plan(cz)

    rim = jnp.zeros((REACH, nx, ny), f32)
    vbuf[:REACH] = rim
    vbuf[REACH + cz :] = rim

    sends = []
    for distance, count in plan:
        sends.append((distance, cz - count, count, REACH - (distance - 1) * cz - count))
        sends.append((-distance, 0, count, REACH + distance * cz))

    def inside(index):
        return jnp.logical_and(index >= 0, index < slabs)

    loads = [
        pltpu.make_async_copy(source, target, load_sem.at[at])
        for at, (source, target) in enumerate(
            [
                (vol_hbm, vbuf.at[pl.ds(REACH, cz)]),
                (w2_hbm, w2_ref),
                (w1_hbm, w1_ref),
                (b1_hbm, b1_ref),
                (b2_hbm, b2_ref),
                (hw_hbm, hw_ref),
                (hb_hbm, hb_ref),
                (mg_hbm, mg_ref),
            ]
        )
    ]
    for load in loads:
        load.start()
    barrier = pltpu.get_barrier_semaphore()
    expected = jnp.int32(0)
    for offset, _, _, _ in sends:
        there = inside(pos + offset)
        expected = expected + there.astype(jnp.int32)

        @pl.when(there)
        def _():
            pl.semaphore_signal(
                barrier, inc=1, device_id={"slab": pos + offset}, device_id_type=MESH
            )

    loads[0].wait()
    pl.semaphore_wait(barrier, expected)

    def copy_of(at):
        offset, first, count, slot = sends[at]
        return pltpu.make_async_remote_copy(
            src_ref=vbuf.at[pl.ds(REACH + first, count)],
            dst_ref=vbuf.at[pl.ds(slot, count)],
            send_sem=send_sem.at[at],
            recv_sem=recv_sem.at[at],
            device_id={"slab": pos + offset},
            device_id_type=MESH,
        )

    for at, (offset, _, _, _) in enumerate(sends):

        @pl.when(inside(pos + offset))
        def _():
            copy_of(at).start()

    for load in loads[1:]:
        load.wait()

    spread = (jnp.bitwise_and(iota((ch, lanes), 1), ch - 1) == iota((ch, lanes), 0)).astype(f32)
    b1 = exact_mm(b1_ref[...].reshape(1, ch), spread)
    b2 = exact_mm(b2_ref[...].reshape(1, ch), spread)
    w1_rows = exact_mm(w1_ref[...].T, spread)
    out_col = iota((ch, lanes), 1) // ch
    in_col = iota((ny, lanes), 0)
    col_gap = in_col - iota((ny, lanes), 1) // ch + 1
    first_parts = []
    for a in range(3):
        part = jnp.zeros((ny, lanes), f32)
        for b in range(3):
            row = w1_rows[3 * a + b : 3 * a + b + 1]
            part = jnp.where(col_gap == b, row, part)
        first_parts.append(part)
    first_w = split(jnp.concatenate(first_parts, axis=0))

    w2_t = w2_ref[...].reshape(9 * ch, ch).T
    spread_b = spread.astype(bf16)
    second_w = []
    for a in range(3):
        tiles = []
        for b in range(3):
            tap = 3 * a + b
            tiles.append([mm(v, spread_b) for v in split(w2_t[:, tap * ch : (tap + 1) * ch])])
        halves = []
        for half in range(2):
            rows = []
            for col in range(ny):
                block = jnp.where(out_col == col + 1, tiles[0][half], 0.0)
                block = jnp.where(out_col == col, tiles[1][half], block)
                block = jnp.where(out_col == col - 1, tiles[2][half], block)
                rows.append(block)
            halves.append(jnp.concatenate(rows, axis=0).astype(bf16))
        second_w.append(tuple(halves))

    hw_rows = exact_mm(hw_ref[...], spread)
    same = iota((ny, lanes), 0) == iota((ny, lanes), 1) // ch
    head_w = split(
        jnp.concatenate(
            [jnp.where(same, hw_rows[k : k + 1], 0.0) for k in range(heads)], axis=0
        )
    )

    for at, (offset, _, _, _) in enumerate(sends):

        @pl.when(inside(pos - offset))
        def _():
            copy_of(at).wait_recv()

    vol = vbuf[...].reshape(zi * nx, ny)
    vol_t = vol.T
    taps_yz = jnp.concatenate([vol[a * nx : (a + zf) * nx] for a in range(3)], axis=1)
    taps_xz = jnp.concatenate([vol_t[:, j * nx : (j + 3) * nx] for j in range(zf)], axis=0)
    row_x = jnp.bitwise_and(iota((zo * nx, ny), 0), nx - 1)
    mid = vol[2 * nx : (2 + zo) * nx]
    above = jnp.where(row_x == 0, 0.0, vol[2 * nx - 1 : (2 + zo) * nx - 1])
    below = jnp.where(row_x == nx - 1, 0.0, vol[2 * nx + 1 : (2 + zo) * nx + 1])
    taps_xy = jnp.concatenate([above, mid, below], axis=1)
    taps = split(jnp.concatenate([taps_xy, taps_xz, taps_yz], axis=0))
    hidden = jnp.maximum(product(mm, taps, first_w) + b1, 0.0)

    at_xz, at_yz, at_end = zo * nx, zo * nx + zf * ny, zo * nx + zf * ny + zf * nx
    slice_of = iota((zf * nx, lanes), 0) // nx + (pos * cz - 2)
    valid = jnp.logical_and(slice_of >= 0, slice_of < slabs * cz)
    hid_xz = split(jnp.where(valid, hidden[at_xz:at_yz], 0.0))
    hid_yz = split(jnp.where(valid, hidden[at_yz:at_end], 0.0))

    pad_ref[:, 0:8] = jnp.zeros((zo, 8, lanes), f32)
    pad_ref[:, nx + 8 : nx + 16] = jnp.zeros((zo, 8, lanes), f32)
    pad_ref[:, 8 : nx + 8] = hidden[:at_xz].reshape(zo, nx, lanes)

    summed = b2
    for a in range(3):
        hid_xy = split(pad_ref[:, 7 + a : 7 + a + nx].reshape(zo * nx, lanes))
        rows = tuple(
            jnp.concatenate(
                [
                    hid_xy[half],
                    hid_xz[half][a * ny : (a + zo) * ny],
                    hid_yz[half][a * nx : (a + zo) * nx],
                ],
                axis=0,
            )
            for half in range(2)
        )
        summed = summed + product(mm, rows, second_w[a])
    feats = split(jnp.maximum(summed, 0.0))
    f_xy, f_xz, f_yz = (
        tuple(v[j * zo * nx : (j + 1) * zo * nx] for v in feats) for j in range(3)
    )

    p_xy = product(mm_nt, f_xy, head_w)
    p_yz = product(mm_nt, f_yz, head_w)
    p_xz = product(mm_nt, head_w, f_xz)
    for k in range(heads):
        bias = hb_ref[k]
        w_xy, w_xz, w_yz = mg_ref[0, k], mg_ref[1, k], mg_ref[2, k]
        cols = slice(k * ny, (k + 1) * ny)
        merged = []
        flat = w_xy * (p_xy[:, cols] + bias) + w_yz * (p_yz[:, cols] + bias)
        side = w_xz * (p_xz[cols] + bias)
        for z in range(zo):
            merged.append(flat[z * nx : (z + 1) * nx] + side[:, z * ny : (z + 1) * ny])
        merged[0] = jnp.where(pos == 0, merged[1], merged[0])
        merged[-1] = jnp.where(pos == slabs - 1, merged[-2], merged[-1])
        for z in range(cz):
            out_ref[k, z] = median_three(merged[z], merged[z + 1], merged[z + 2])

    for at, (offset, _, _, _) in enumerate(sends):

        @pl.when(inside(pos + offset))
        def _():
            copy_of(at).wait_send()


def on_device_small(volume, *params):
    cz, nx, ny = volume.shape
    ch = params[0].shape[0]
    heads = params[4].shape[0]
    slabs = lax.axis_size("slab")
    copies = 2 * len(halo_plan(cz))
    return pl.pallas_call(
        lambda *refs: brick_kernel(slabs, *refs),
        out_shape=pltpu.VMEM((heads, cz, nx, ny), f32),
        in_specs=[pl.BlockSpec(memory_space=pltpu.HBM)] * 8,
        out_specs=pl.BlockSpec(memory_space=pltpu.VMEM),
        scratch_shapes=[
            pltpu.VMEM((cz + 2 * REACH, nx, ny), f32),
            *[pltpu.VMEM(param.shape, f32) for param in params[:5]],
            *[pltpu.SMEM(param.shape, f32) for param in params[5:]],
            pltpu.VMEM((cz + 2, nx + 16, ny * ch), f32),
            pltpu.SemaphoreType.DMA((copies,)),
            pltpu.SemaphoreType.DMA((copies,)),
            pltpu.SemaphoreType.DMA((8,)),
        ],
        compiler_params=pltpu.CompilerParams(
            collective_id=0, has_side_effects=True
        ),
        name="brick",
    )(volume, *params)


def on_device_any(volume, *params):
    _, nx, ny = volume.shape
    ch = params[0].shape[0]
    if nx == ny and nx % 16 == 0 and ch % 16 == 0 and nx & (nx - 1) == 0 and ch & (ch - 1) == 0:
        if ny * ch <= 512:
            return on_device_small(volume, *params)
    return on_device(volume, *params)


def solution(mesh):
    in_specs = (P(("groups", "slab"), None, None), P(), P(), P(), P(), P(), P(), P())
    out_specs = P(None, ("groups", "slab"), None, None)
    return jax.shard_map(
        on_device_any, mesh=mesh, in_specs=in_specs, out_specs=out_specs, check_vma=False
    )
```

```python
import jax
import jax.numpy as jnp
from jax import lax
from jax.experimental import pallas as pl
from jax.experimental.pallas import tpu as pltpu
from jax.sharding import PartitionSpec as P

exact_prec = lax.Precision.HIGHEST


def with_halo(block, sides, width):
    for axis, dim in sides:
        count = lax.axis_size(axis)
        forward = [(i, i + 1) for i in range(count - 1)]
        backward = [(target, source) for source, target in forward]
        low = lax.ppermute(
            lax.slice_in_dim(block, block.shape[dim] - width, None, axis=dim), axis, forward
        )
        high = lax.ppermute(lax.slice_in_dim(block, 0, width, axis=dim), axis, backward)
        block = jnp.concatenate([low, block, high], axis=dim)
    return block


def plane_features(planes, conv_first, first_bias, conv_second, second_bias):
    rows_in = planes.shape[1]
    cols_in = planes.shape[2]
    padded = jnp.pad(planes, ((0, 0), (1, 1), (1, 1)))
    tap_stack = jnp.stack(
        [
            padded[:, row_off : row_off + rows_in, col_off : col_off + cols_in]
            for row_off in range(3)
            for col_off in range(3)
        ]
    )
    hidden_one = (
        jnp.einsum("ct,tbhw->cbhw", conv_first, tap_stack, precision=exact_prec)
        + first_bias[:, None, None, None]
    )
    hidden_one = jnp.maximum(hidden_one, 0.0)
    padded_one = jnp.pad(hidden_one, ((0, 0), (0, 0), (1, 1), (1, 1)))
    summed = jnp.zeros(hidden_one.shape, jnp.float32) + second_bias[:, None, None, None]
    for row_off in range(3):
        for col_off in range(3):
            window = padded_one[:, :, row_off : row_off + rows_in, col_off : col_off + cols_in]
            summed = summed + jnp.einsum(
                "oi,ibhw->obhw", conv_second[3 * row_off + col_off], window, precision=exact_prec
            )
    return jnp.maximum(summed, 0.0)


def apply_heads(features, head_weight, head_bias):
    return (
        jnp.einsum("ko,obhw->kbhw", head_weight, features, precision=exact_prec)
        + head_bias[:, None, None, None]
    )


def median_three(lower_side, middle, upper_side):
    return jnp.maximum(
        jnp.minimum(lower_side, middle), jnp.minimum(jnp.maximum(lower_side, middle), upper_side)
    )


def predict_each(planes, conv_first, first_bias, conv_second, second_bias, head_weight, head_bias):

    def one_plane(single):
        features = plane_features(single[None], conv_first, first_bias, conv_second, second_bias)
        return apply_heads(features, head_weight, head_bias)[:, 0]

    result = lax.map(one_plane, planes)
    return jnp.transpose(result, (1, 0, 2, 3))


def on_device(
    volume, conv_first, first_bias, conv_second, second_bias, head_weight, head_bias, merging
):
    slab_count = lax.axis_size("slab")
    position = lax.axis_index("slab")
    across_y, across_x = (
        lax.all_to_all(
            jnp.transpose(volume, (2, 0, 1)), "slab", split_axis=0, concat_axis=1, tiled=True
        ),
        lax.all_to_all(
            jnp.transpose(volume, (1, 0, 2)), "slab", split_axis=0, concat_axis=1, tiled=True
        ),
    )
    xy_pred = predict_each(
        volume, conv_first, first_bias, conv_second, second_bias, head_weight, head_bias
    )
    xz_load = predict_each(
        across_y, conv_first, first_bias, conv_second, second_bias, head_weight, head_bias
    )
    yz_load = predict_each(
        across_x, conv_first, first_bias, conv_second, second_bias, head_weight, head_bias
    )
    xz_back = lax.all_to_all(xz_load, "slab", split_axis=2, concat_axis=1, tiled=True)
    yz_back = lax.all_to_all(yz_load, "slab", split_axis=2, concat_axis=1, tiled=True)
    xz_pred = jnp.transpose(xz_back, (0, 2, 3, 1))
    yz_pred = jnp.transpose(yz_back, (0, 2, 1, 3))
    merged_pred = (
        merging[0][:, None, None, None] * xy_pred
        + merging[1][:, None, None, None] * xz_pred
        + merging[2][:, None, None, None] * yz_pred
    )
    padded = with_halo(merged_pred, (("slab", 1),), 1)
    under_rim = jnp.where(position == 0, merged_pred[:, :1], padded[:, :1])
    over_rim = jnp.where(position == slab_count - 1, merged_pred[:, -1:], padded[:, -1:])
    lower_side = jnp.concatenate([under_rim, merged_pred[:, :-1]], axis=1)
    upper_side = jnp.concatenate([merged_pred[:, 1:], over_rim], axis=1)
    return median_three(lower_side, merged_pred, upper_side)


MESH = pl.DeviceIdType.MESH
f32 = jnp.float32
bf16 = jnp.bfloat16
REACH = 3


def split(x):
    hi = x.astype(bf16)
    return hi, (x - hi.astype(f32)).astype(bf16)


def mm(a, b):
    return lax.dot_general(a, b, (((1,), (0,)), ((), ())), preferred_element_type=f32)


def mm_nt(a, b):
    return lax.dot_general(a, b, (((1,), (1,)), ((), ())), preferred_element_type=f32)


def exact_mm(a, b):
    return lax.dot_general(
        a, b, (((1,), (0,)), ((), ())), preferred_element_type=f32, precision=exact_prec
    )


def product(mul, a, b):
    (a_hi, a_lo), (b_hi, b_lo) = a, b
    if mul is mm:
        return mul(
            jnp.concatenate([a_hi, a_lo, a_hi], axis=1),
            jnp.concatenate([b_hi, b_hi, b_lo], axis=0),
        )
    return mul(a_hi, b_hi) + (mul(a_hi, b_lo) + mul(a_lo, b_hi))


def iota(shape, dim):
    return lax.broadcasted_iota(jnp.int32, shape, dim)


def halo_plan(cz):
    plan = []
    left = REACH
    distance = 1
    while left > 0:
        count = min(cz, left)
        plan.append((distance, count))
        left -= count
        distance += 1
    return plan


def brick_kernel(
    slabs,
    vol_hbm,
    w1_hbm,
    b1_hbm,
    w2_hbm,
    b2_hbm,
    hw_hbm,
    hb_hbm,
    mg_hbm,
    out_ref,
    vbuf,
    w1_ref,
    b1_ref,
    w2_ref,
    b2_ref,
    hw_ref,
    hb_ref,
    mg_ref,
    pad_ref,
    send_sem,
    recv_sem,
    load_sem,
):
    cz, nx, ny = vol_hbm.shape
    ch = w1_ref.shape[0]
    heads = hw_ref.shape[0]
    lanes = ny * ch
    zi, zf, zo = cz + 6, cz + 4, cz + 2
    pos = lax.axis_index("slab")
    plan = halo_plan(cz)

    rim = jnp.zeros((REACH, nx, ny), f32)
    vbuf[:REACH] = rim
    vbuf[REACH + cz :] = rim

    sends = []
    for distance, count in plan[::-1]:
        sends.append((distance, cz - count, count, REACH - (distance - 1) * cz - count))
        sends.append((-distance, 0, count, REACH + distance * cz))

    def inside(index):
        return jnp.logical_and(index >= 0, index < slabs)

    loads = [
        pltpu.make_async_copy(source, target, load_sem.at[at])
        for at, (source, target) in enumerate(
            [
                (vol_hbm, vbuf.at[pl.ds(REACH, cz)]),
                (w2_hbm, w2_ref),
                (w1_hbm, w1_ref),
                (b1_hbm, b1_ref),
                (b2_hbm, b2_ref),
                (hw_hbm, hw_ref),
                (hb_hbm, hb_ref),
                (mg_hbm, mg_ref),
            ]
        )
    ]
    for load in loads:
        load.start()
    barrier = pltpu.get_barrier_semaphore()
    expected = jnp.int32(0)
    for offset, _, _, _ in sends:
        there = inside(pos + offset)
        expected = expected + there.astype(jnp.int32)

        @pl.when(there)
        def _():
            pl.semaphore_signal(
                barrier, inc=1, device_id={"slab": pos + offset}, device_id_type=MESH
            )

    loads[0].wait()
    pl.semaphore_wait(barrier, expected)

    def copy_of(at):
        offset, first, count, slot = sends[at]
        return pltpu.make_async_remote_copy(
            src_ref=vbuf.at[pl.ds(REACH + first, count)],
            dst_ref=vbuf.at[pl.ds(slot, count)],
            send_sem=send_sem.at[at],
            recv_sem=recv_sem.at[at],
            device_id={"slab": pos + offset},
            device_id_type=MESH,
        )

    for at, (offset, _, _, _) in enumerate(sends):

        @pl.when(inside(pos + offset))
        def _():
            copy_of(at).start()

    for load in loads[1:]:
        load.wait()

    spread = (jnp.bitwise_and(iota((ch, lanes), 1), ch - 1) == iota((ch, lanes), 0)).astype(f32)
    b1 = exact_mm(b1_ref[...].reshape(1, ch), spread)
    b2 = exact_mm(b2_ref[...].reshape(1, ch), spread)
    w1_rows = exact_mm(w1_ref[...].T, spread)
    out_col = iota((ch, lanes), 1) // ch
    in_col = iota((ny, lanes), 0)
    col_gap = in_col - iota((ny, lanes), 1) // ch + 1
    first_parts = []
    for a in range(3):
        part = jnp.zeros((ny, lanes), f32)
        for b in range(3):
            row = w1_rows[3 * a + b : 3 * a + b + 1]
            part = jnp.where(col_gap == b, row, part)
        first_parts.append(part)
    first_w = split(jnp.concatenate(first_parts, axis=0))

    w2_t = w2_ref[...].reshape(9 * ch, ch).T
    spread_b = spread.astype(bf16)
    second_w = []
    for a in range(3):
        tiles = []
        for b in range(3):
            tap = 3 * a + b
            tiles.append([mm(v, spread_b) for v in split(w2_t[:, tap * ch : (tap + 1) * ch])])
        halves = []
        for half in range(2):
            rows = []
            for col in range(ny):
                block = jnp.where(out_col == col + 1, tiles[0][half], 0.0)
                block = jnp.where(out_col == col, tiles[1][half], block)
                block = jnp.where(out_col == col - 1, tiles[2][half], block)
                rows.append(block)
            halves.append(jnp.concatenate(rows, axis=0).astype(bf16))
        second_w.append(tuple(halves))

    hw_rows = exact_mm(hw_ref[...], spread)
    same = iota((ny, lanes), 0) == iota((ny, lanes), 1) // ch
    head_w = split(
        jnp.concatenate(
            [jnp.where(same, hw_rows[k : k + 1], 0.0) for k in range(heads)], axis=0
        )
    )

    for at, (offset, _, _, _) in enumerate(sends):

        @pl.when(inside(pos - offset))
        def _():
            copy_of(at).wait_recv()

    vol = vbuf[...].reshape(zi * nx, ny)
    vol_t = vol.T
    taps_yz = jnp.concatenate([vol[a * nx : (a + zf) * nx] for a in range(3)], axis=1)
    taps_xz = jnp.concatenate([vol_t[:, j * nx : (j + 3) * nx] for j in range(zf)], axis=0)
    row_x = jnp.bitwise_and(iota((zo * nx, ny), 0), nx - 1)
    mid = vol[2 * nx : (2 + zo) * nx]
    above = jnp.where(row_x == 0, 0.0, vol[2 * nx - 1 : (2 + zo) * nx - 1])
    below = jnp.where(row_x == nx - 1, 0.0, vol[2 * nx + 1 : (2 + zo) * nx + 1])
    taps_xy = jnp.concatenate([above, mid, below], axis=1)
    taps = split(jnp.concatenate([taps_xy, taps_xz, taps_yz], axis=0))
    hidden = jnp.maximum(product(mm, taps, first_w) + b1, 0.0)

    at_xz, at_yz, at_end = zo * nx, zo * nx + zf * ny, zo * nx + zf * ny + zf * nx
    slice_of = iota((zf * nx, lanes), 0) // nx + (pos * cz - 2)
    valid = jnp.logical_and(slice_of >= 0, slice_of < slabs * cz)
    hid_xz = split(jnp.where(valid, hidden[at_xz:at_yz], 0.0))
    hid_yz = split(jnp.where(valid, hidden[at_yz:at_end], 0.0))

    pad_ref[:, 0:8] = jnp.zeros((zo, 8, lanes), f32)
    pad_ref[:, nx + 8 : nx + 16] = jnp.zeros((zo, 8, lanes), f32)
    pad_ref[:, 8 : nx + 8] = hidden[:at_xz].reshape(zo, nx, lanes)

    summed = b2
    for a in range(3):
        hid_xy = split(pad_ref[:, 7 + a : 7 + a + nx].reshape(zo * nx, lanes))
        rows = tuple(
            jnp.concatenate(
                [
                    hid_xy[half],
                    hid_xz[half][a * ny : (a + zo) * ny],
                    hid_yz[half][a * nx : (a + zo) * nx],
                ],
                axis=0,
            )
            for half in range(2)
        )
        summed = summed + product(mm, rows, second_w[a])
    feats = split(jnp.maximum(summed, 0.0))
    f_xy, f_xz, f_yz = (
        tuple(v[j * zo * nx : (j + 1) * zo * nx] for v in feats) for j in range(3)
    )

    p_xy = product(mm_nt, f_xy, head_w)
    p_yz = product(mm_nt, f_yz, head_w)
    p_xz = product(mm_nt, head_w, f_xz)
    for k in range(heads):
        bias = hb_ref[k]
        w_xy, w_xz, w_yz = mg_ref[0, k], mg_ref[1, k], mg_ref[2, k]
        cols = slice(k * ny, (k + 1) * ny)
        merged = []
        flat = w_xy * (p_xy[:, cols] + bias) + w_yz * (p_yz[:, cols] + bias)
        side = w_xz * (p_xz[cols] + bias)
        for z in range(zo):
            merged.append(flat[z * nx : (z + 1) * nx] + side[:, z * ny : (z + 1) * ny])
        merged[0] = jnp.where(pos == 0, merged[1], merged[0])
        merged[-1] = jnp.where(pos == slabs - 1, merged[-2], merged[-1])
        for z in range(cz):
            out_ref[k, z] = median_three(merged[z], merged[z + 1], merged[z + 2])

    for at, (offset, _, _, _) in enumerate(sends):

        @pl.when(inside(pos + offset))
        def _():
            copy_of(at).wait_send()


def on_device_small(volume, *params):
    cz, nx, ny = volume.shape
    ch = params[0].shape[0]
    heads = params[4].shape[0]
    slabs = lax.axis_size("slab")
    copies = 2 * len(halo_plan(cz))
    return pl.pallas_call(
        lambda *refs: brick_kernel(slabs, *refs),
        out_shape=pltpu.VMEM((heads, cz, nx, ny), f32),
        in_specs=[pl.BlockSpec(memory_space=pltpu.HBM)] * 8,
        out_specs=pl.BlockSpec(memory_space=pltpu.VMEM),
        scratch_shapes=[
            pltpu.VMEM((cz + 2 * REACH, nx, ny), f32),
            *[pltpu.VMEM(param.shape, f32) for param in params[:5]],
            *[pltpu.SMEM(param.shape, f32) for param in params[5:]],
            pltpu.VMEM((cz + 2, nx + 16, ny * ch), f32),
            pltpu.SemaphoreType.DMA((copies,)),
            pltpu.SemaphoreType.DMA((copies,)),
            pltpu.SemaphoreType.DMA((8,)),
        ],
        compiler_params=pltpu.CompilerParams(
            collective_id=0, has_side_effects=True
        ),
        name="brick",
    )(volume, *params)


def on_device_any(volume, *params):
    _, nx, ny = volume.shape
    ch = params[0].shape[0]
    if nx == ny and nx % 16 == 0 and ch % 16 == 0 and nx & (nx - 1) == 0 and ch & (ch - 1) == 0:
        if ny * ch <= 512:
            return on_device_small(volume, *params)
    return on_device(volume, *params)


def solution(mesh):
    in_specs = (P(("groups", "slab"), None, None), P(), P(), P(), P(), P(), P(), P())
    out_specs = P(None, ("groups", "slab"), None, None)
    return jax.shard_map(
        on_device_any, mesh=mesh, in_specs=in_specs, out_specs=out_specs, check_vma=False
    )
```

```python
import jax
import jax.numpy as jnp
from jax import lax
from jax.experimental import pallas as pl
from jax.experimental.pallas import tpu as pltpu
from jax.sharding import PartitionSpec as P

exact_prec = lax.Precision.HIGHEST


def with_halo(block, sides, width):
    for axis, dim in sides:
        count = lax.axis_size(axis)
        forward = [(i, i + 1) for i in range(count - 1)]
        backward = [(target, source) for source, target in forward]
        low = lax.ppermute(
            lax.slice_in_dim(block, block.shape[dim] - width, None, axis=dim), axis, forward
        )
        high = lax.ppermute(lax.slice_in_dim(block, 0, width, axis=dim), axis, backward)
        block = jnp.concatenate([low, block, high], axis=dim)
    return block


def plane_features(planes, conv_first, first_bias, conv_second, second_bias):
    rows_in = planes.shape[1]
    cols_in = planes.shape[2]
    padded = jnp.pad(planes, ((0, 0), (1, 1), (1, 1)))
    tap_stack = jnp.stack(
        [
            padded[:, row_off : row_off + rows_in, col_off : col_off + cols_in]
            for row_off in range(3)
            for col_off in range(3)
        ]
    )
    hidden_one = (
        jnp.einsum("ct,tbhw->cbhw", conv_first, tap_stack, precision=exact_prec)
        + first_bias[:, None, None, None]
    )
    hidden_one = jnp.maximum(hidden_one, 0.0)
    padded_one = jnp.pad(hidden_one, ((0, 0), (0, 0), (1, 1), (1, 1)))
    summed = jnp.zeros(hidden_one.shape, jnp.float32) + second_bias[:, None, None, None]
    for row_off in range(3):
        for col_off in range(3):
            window = padded_one[:, :, row_off : row_off + rows_in, col_off : col_off + cols_in]
            summed = summed + jnp.einsum(
                "oi,ibhw->obhw", conv_second[3 * row_off + col_off], window, precision=exact_prec
            )
    return jnp.maximum(summed, 0.0)


def apply_heads(features, head_weight, head_bias):
    return (
        jnp.einsum("ko,obhw->kbhw", head_weight, features, precision=exact_prec)
        + head_bias[:, None, None, None]
    )


def median_three(lower_side, middle, upper_side):
    return jnp.maximum(
        jnp.minimum(lower_side, middle), jnp.minimum(jnp.maximum(lower_side, middle), upper_side)
    )


def predict_each(planes, conv_first, first_bias, conv_second, second_bias, head_weight, head_bias):

    def one_plane(single):
        features = plane_features(single[None], conv_first, first_bias, conv_second, second_bias)
        return apply_heads(features, head_weight, head_bias)[:, 0]

    result = lax.map(one_plane, planes)
    return jnp.transpose(result, (1, 0, 2, 3))


def on_device(
    volume, conv_first, first_bias, conv_second, second_bias, head_weight, head_bias, merging
):
    slab_count = lax.axis_size("slab")
    position = lax.axis_index("slab")
    across_y, across_x = (
        lax.all_to_all(
            jnp.transpose(volume, (2, 0, 1)), "slab", split_axis=0, concat_axis=1, tiled=True
        ),
        lax.all_to_all(
            jnp.transpose(volume, (1, 0, 2)), "slab", split_axis=0, concat_axis=1, tiled=True
        ),
    )
    xy_pred = predict_each(
        volume, conv_first, first_bias, conv_second, second_bias, head_weight, head_bias
    )
    xz_load = predict_each(
        across_y, conv_first, first_bias, conv_second, second_bias, head_weight, head_bias
    )
    yz_load = predict_each(
        across_x, conv_first, first_bias, conv_second, second_bias, head_weight, head_bias
    )
    xz_back = lax.all_to_all(xz_load, "slab", split_axis=2, concat_axis=1, tiled=True)
    yz_back = lax.all_to_all(yz_load, "slab", split_axis=2, concat_axis=1, tiled=True)
    xz_pred = jnp.transpose(xz_back, (0, 2, 3, 1))
    yz_pred = jnp.transpose(yz_back, (0, 2, 1, 3))
    merged_pred = (
        merging[0][:, None, None, None] * xy_pred
        + merging[1][:, None, None, None] * xz_pred
        + merging[2][:, None, None, None] * yz_pred
    )
    padded = with_halo(merged_pred, (("slab", 1),), 1)
    under_rim = jnp.where(position == 0, merged_pred[:, :1], padded[:, :1])
    over_rim = jnp.where(position == slab_count - 1, merged_pred[:, -1:], padded[:, -1:])
    lower_side = jnp.concatenate([under_rim, merged_pred[:, :-1]], axis=1)
    upper_side = jnp.concatenate([merged_pred[:, 1:], over_rim], axis=1)
    return median_three(lower_side, merged_pred, upper_side)


MESH = pl.DeviceIdType.MESH
f32 = jnp.float32
bf16 = jnp.bfloat16
REACH = 3


def split(x):
    hi = x.astype(bf16)
    return hi, (x - hi.astype(f32)).astype(bf16)


def mm(a, b):
    return lax.dot_general(a, b, (((1,), (0,)), ((), ())), preferred_element_type=f32)


def mm_nt(a, b):
    return lax.dot_general(a, b, (((1,), (1,)), ((), ())), preferred_element_type=f32)


def exact_mm(a, b):
    return lax.dot_general(
        a, b, (((1,), (0,)), ((), ())), preferred_element_type=f32, precision=exact_prec
    )


def product(mul, a, b):
    (a_hi, a_lo), (b_hi, b_lo) = a, b
    if mul is mm:
        return mul(
            jnp.concatenate([a_hi, a_lo, a_hi], axis=1),
            jnp.concatenate([b_hi, b_hi, b_lo], axis=0),
        )
    return mul(a_hi, b_hi) + (mul(a_hi, b_lo) + mul(a_lo, b_hi))


def iota(shape, dim):
    return lax.broadcasted_iota(jnp.int32, shape, dim)


def halo_plan(cz):
    plan = []
    left = REACH
    distance = 1
    while left > 0:
        count = min(cz, left)
        plan.append((distance, count))
        left -= count
        distance += 1
    return plan


def brick_kernel(
    slabs,
    vol_hbm,
    w1_hbm,
    b1_hbm,
    w2_hbm,
    b2_hbm,
    hw_hbm,
    hb_hbm,
    mg_hbm,
    out_ref,
    vbuf,
    w1_ref,
    b1_ref,
    w2_ref,
    b2_ref,
    hw_ref,
    hb_ref,
    mg_ref,
    pad_ref,
    send_sem,
    recv_sem,
    load_sem,
):
    cz, nx, ny = vol_hbm.shape
    ch = w1_ref.shape[0]
    heads = hw_ref.shape[0]
    lanes = ny * ch
    zi, zf, zo = cz + 6, cz + 4, cz + 2
    pos = lax.axis_index("slab")
    plan = halo_plan(cz)

    rim = jnp.zeros((REACH, nx, ny), f32)
    vbuf[:REACH] = rim
    vbuf[REACH + cz :] = rim

    sends = []
    for distance, count in plan[::-1]:
        sends.append((distance, cz - count, count, REACH - (distance - 1) * cz - count))
        sends.append((-distance, 0, count, REACH + distance * cz))

    def inside(index):
        return jnp.logical_and(index >= 0, index < slabs)

    loads = [
        pltpu.make_async_copy(source, target, load_sem.at[at])
        for at, (source, target) in enumerate(
            [
                (vol_hbm, vbuf.at[pl.ds(REACH, cz)]),
                (w2_hbm, w2_ref),
                (w1_hbm, w1_ref),
                (b1_hbm, b1_ref),
                (b2_hbm, b2_ref),
                (hw_hbm, hw_ref),
                (hb_hbm, hb_ref),
                (mg_hbm, mg_ref),
            ]
        )
    ]
    loads[0].start()
    barrier = pltpu.get_barrier_semaphore()
    expected = jnp.int32(0)
    for offset, _, _, _ in sends:
        there = inside(pos + offset)
        expected = expected + there.astype(jnp.int32)

        @pl.when(there)
        def _():
            pl.semaphore_signal(
                barrier, inc=1, device_id={"slab": pos + offset}, device_id_type=MESH
            )

    for load in loads[1:]:
        load.start()
    loads[0].wait()
    pl.semaphore_wait(barrier, expected)

    def copy_of(at):
        offset, first, count, slot = sends[at]
        return pltpu.make_async_remote_copy(
            src_ref=vbuf.at[pl.ds(REACH + first, count)],
            dst_ref=vbuf.at[pl.ds(slot, count)],
            send_sem=send_sem.at[at],
            recv_sem=recv_sem.at[at],
            device_id={"slab": pos + offset},
            device_id_type=MESH,
        )

    for at, (offset, _, _, _) in enumerate(sends):

        @pl.when(inside(pos + offset))
        def _():
            copy_of(at).start()

    for load in loads[1:]:
        load.wait()

    spread = (jnp.bitwise_and(iota((ch, lanes), 1), ch - 1) == iota((ch, lanes), 0)).astype(f32)
    b1 = exact_mm(b1_ref[...].reshape(1, ch), spread)
    b2 = exact_mm(b2_ref[...].reshape(1, ch), spread)
    w1_rows = exact_mm(w1_ref[...].T, spread)
    out_col = iota((ch, lanes), 1) // ch
    in_col = iota((ny, lanes), 0)
    col_gap = in_col - iota((ny, lanes), 1) // ch + 1
    first_parts = []
    for a in range(3):
        part = jnp.zeros((ny, lanes), f32)
        for b in range(3):
            row = w1_rows[3 * a + b : 3 * a + b + 1]
            part = jnp.where(col_gap == b, row, part)
        first_parts.append(part)
    first_w = split(jnp.concatenate(first_parts, axis=0))

    w2_t = w2_ref[...].reshape(9 * ch, ch).T
    spread_b = spread.astype(bf16)
    second_w = []
    for a in range(3):
        tiles = []
        for b in range(3):
            tap = 3 * a + b
            tiles.append([mm(v, spread_b) for v in split(w2_t[:, tap * ch : (tap + 1) * ch])])
        halves = []
        for half in range(2):
            rows = []
            for col in range(ny):
                block = jnp.where(out_col == col + 1, tiles[0][half], 0.0)
                block = jnp.where(out_col == col, tiles[1][half], block)
                block = jnp.where(out_col == col - 1, tiles[2][half], block)
                rows.append(block)
            halves.append(jnp.concatenate(rows, axis=0).astype(bf16))
        second_w.append(tuple(halves))

    hw_rows = exact_mm(hw_ref[...], spread)
    same = iota((ny, lanes), 0) == iota((ny, lanes), 1) // ch
    head_w = split(
        jnp.concatenate(
            [jnp.where(same, hw_rows[k : k + 1], 0.0) for k in range(heads)], axis=0
        )
    )

    for at, (offset, _, _, _) in enumerate(sends):

        @pl.when(inside(pos - offset))
        def _():
            copy_of(at).wait_recv()

    vol = vbuf[...].reshape(zi * nx, ny)
    vol_t = vol.T
    taps_yz = jnp.concatenate([vol[a * nx : (a + zf) * nx] for a in range(3)], axis=1)
    taps_xz = jnp.concatenate([vol_t[:, j * nx : (j + 3) * nx] for j in range(zf)], axis=0)
    row_x = jnp.bitwise_and(iota((zo * nx, ny), 0), nx - 1)
    mid = vol[2 * nx : (2 + zo) * nx]
    above = jnp.where(row_x == 0, 0.0, vol[2 * nx - 1 : (2 + zo) * nx - 1])
    below = jnp.where(row_x == nx - 1, 0.0, vol[2 * nx + 1 : (2 + zo) * nx + 1])
    taps_xy = jnp.concatenate([above, mid, below], axis=1)
    taps = split(jnp.concatenate([taps_xy, taps_xz, taps_yz], axis=0))
    hidden = jnp.maximum(product(mm, taps, first_w) + b1, 0.0)

    at_xz, at_yz, at_end = zo * nx, zo * nx + zf * ny, zo * nx + zf * ny + zf * nx
    slice_of = iota((zf * nx, lanes), 0) // nx + (pos * cz - 2)
    valid = jnp.logical_and(slice_of >= 0, slice_of < slabs * cz)
    hid_xz = split(jnp.where(valid, hidden[at_xz:at_yz], 0.0))
    hid_yz = split(jnp.where(valid, hidden[at_yz:at_end], 0.0))

    pad_ref[:, 0:8] = jnp.zeros((zo, 8, lanes), f32)
    pad_ref[:, nx + 8 : nx + 16] = jnp.zeros((zo, 8, lanes), f32)
    pad_ref[:, 8 : nx + 8] = hidden[:at_xz].reshape(zo, nx, lanes)

    summed = b2
    for a in range(3):
        hid_xy = split(pad_ref[:, 7 + a : 7 + a + nx].reshape(zo * nx, lanes))
        rows = tuple(
            jnp.concatenate(
                [
                    hid_xy[half],
                    hid_xz[half][a * ny : (a + zo) * ny],
                    hid_yz[half][a * nx : (a + zo) * nx],
                ],
                axis=0,
            )
            for half in range(2)
        )
        summed = summed + product(mm, rows, second_w[a])
    feats = split(jnp.maximum(summed, 0.0))
    f_xy, f_xz, f_yz = (
        tuple(v[j * zo * nx : (j + 1) * zo * nx] for v in feats) for j in range(3)
    )

    p_xy = product(mm_nt, f_xy, head_w)
    p_yz = product(mm_nt, f_yz, head_w)
    p_xz = product(mm_nt, head_w, f_xz)
    for k in range(heads):
        bias = hb_ref[k]
        w_xy, w_xz, w_yz = mg_ref[0, k], mg_ref[1, k], mg_ref[2, k]
        cols = slice(k * ny, (k + 1) * ny)
        merged = []
        flat = w_xy * (p_xy[:, cols] + bias) + w_yz * (p_yz[:, cols] + bias)
        side = w_xz * (p_xz[cols] + bias)
        for z in range(zo):
            merged.append(flat[z * nx : (z + 1) * nx] + side[:, z * ny : (z + 1) * ny])
        merged[0] = jnp.where(pos == 0, merged[1], merged[0])
        merged[-1] = jnp.where(pos == slabs - 1, merged[-2], merged[-1])
        for z in range(cz):
            out_ref[k, z] = median_three(merged[z], merged[z + 1], merged[z + 2])

    for at, (offset, _, _, _) in enumerate(sends):

        @pl.when(inside(pos + offset))
        def _():
            copy_of(at).wait_send()


def on_device_small(volume, *params):
    cz, nx, ny = volume.shape
    ch = params[0].shape[0]
    heads = params[4].shape[0]
    slabs = lax.axis_size("slab")
    copies = 2 * len(halo_plan(cz))
    return pl.pallas_call(
        lambda *refs: brick_kernel(slabs, *refs),
        out_shape=pltpu.VMEM((heads, cz, nx, ny), f32),
        in_specs=[pl.BlockSpec(memory_space=pltpu.HBM)] * 8,
        out_specs=pl.BlockSpec(memory_space=pltpu.VMEM),
        scratch_shapes=[
            pltpu.VMEM((cz + 2 * REACH, nx, ny), f32),
            *[pltpu.VMEM(param.shape, f32) for param in params[:5]],
            *[pltpu.SMEM(param.shape, f32) for param in params[5:]],
            pltpu.VMEM((cz + 2, nx + 16, ny * ch), f32),
            pltpu.SemaphoreType.DMA((copies,)),
            pltpu.SemaphoreType.DMA((copies,)),
            pltpu.SemaphoreType.DMA((8,)),
        ],
        compiler_params=pltpu.CompilerParams(
            collective_id=0, has_side_effects=True
        ),
        name="brick",
    )(volume, *params)


def on_device_any(volume, *params):
    _, nx, ny = volume.shape
    ch = params[0].shape[0]
    if nx == ny and nx % 16 == 0 and ch % 16 == 0 and nx & (nx - 1) == 0 and ch & (ch - 1) == 0:
        if ny * ch <= 512:
            return on_device_small(volume, *params)
    return on_device(volume, *params)


def solution(mesh):
    in_specs = (P(("groups", "slab"), None, None), P(), P(), P(), P(), P(), P(), P())
    out_specs = P(None, ("groups", "slab"), None, None)
    return jax.shard_map(
        on_device_any, mesh=mesh, in_specs=in_specs, out_specs=out_specs, check_vma=False
    )
```

```python
import jax
import jax.numpy as jnp
from jax import lax
from jax.experimental import pallas as pl
from jax.experimental.pallas import tpu as pltpu
from jax.sharding import PartitionSpec as P

exact_prec = lax.Precision.HIGHEST


def with_halo(block, sides, width):
    for axis, dim in sides:
        count = lax.axis_size(axis)
        forward = [(i, i + 1) for i in range(count - 1)]
        backward = [(target, source) for source, target in forward]
        low = lax.ppermute(
            lax.slice_in_dim(block, block.shape[dim] - width, None, axis=dim), axis, forward
        )
        high = lax.ppermute(lax.slice_in_dim(block, 0, width, axis=dim), axis, backward)
        block = jnp.concatenate([low, block, high], axis=dim)
    return block


def plane_features(planes, conv_first, first_bias, conv_second, second_bias):
    rows_in = planes.shape[1]
    cols_in = planes.shape[2]
    padded = jnp.pad(planes, ((0, 0), (1, 1), (1, 1)))
    tap_stack = jnp.stack(
        [
            padded[:, row_off : row_off + rows_in, col_off : col_off + cols_in]
            for row_off in range(3)
            for col_off in range(3)
        ]
    )
    hidden_one = (
        jnp.einsum("ct,tbhw->cbhw", conv_first, tap_stack, precision=exact_prec)
        + first_bias[:, None, None, None]
    )
    hidden_one = jnp.maximum(hidden_one, 0.0)
    padded_one = jnp.pad(hidden_one, ((0, 0), (0, 0), (1, 1), (1, 1)))
    summed = jnp.zeros(hidden_one.shape, jnp.float32) + second_bias[:, None, None, None]
    for row_off in range(3):
        for col_off in range(3):
            window = padded_one[:, :, row_off : row_off + rows_in, col_off : col_off + cols_in]
            summed = summed + jnp.einsum(
                "oi,ibhw->obhw", conv_second[3 * row_off + col_off], window, precision=exact_prec
            )
    return jnp.maximum(summed, 0.0)


def apply_heads(features, head_weight, head_bias):
    return (
        jnp.einsum("ko,obhw->kbhw", head_weight, features, precision=exact_prec)
        + head_bias[:, None, None, None]
    )


def median_three(lower_side, middle, upper_side):
    return jnp.maximum(
        jnp.minimum(lower_side, middle), jnp.minimum(jnp.maximum(lower_side, middle), upper_side)
    )


def predict_each(planes, conv_first, first_bias, conv_second, second_bias, head_weight, head_bias):

    def one_plane(single):
        features = plane_features(single[None], conv_first, first_bias, conv_second, second_bias)
        return apply_heads(features, head_weight, head_bias)[:, 0]

    result = lax.map(one_plane, planes)
    return jnp.transpose(result, (1, 0, 2, 3))


def on_device(
    volume, conv_first, first_bias, conv_second, second_bias, head_weight, head_bias, merging
):
    slab_count = lax.axis_size("slab")
    position = lax.axis_index("slab")
    across_y, across_x = (
        lax.all_to_all(
            jnp.transpose(volume, (2, 0, 1)), "slab", split_axis=0, concat_axis=1, tiled=True
        ),
        lax.all_to_all(
            jnp.transpose(volume, (1, 0, 2)), "slab", split_axis=0, concat_axis=1, tiled=True
        ),
    )
    xy_pred = predict_each(
        volume, conv_first, first_bias, conv_second, second_bias, head_weight, head_bias
    )
    xz_load = predict_each(
        across_y, conv_first, first_bias, conv_second, second_bias, head_weight, head_bias
    )
    yz_load = predict_each(
        across_x, conv_first, first_bias, conv_second, second_bias, head_weight, head_bias
    )
    xz_back = lax.all_to_all(xz_load, "slab", split_axis=2, concat_axis=1, tiled=True)
    yz_back = lax.all_to_all(yz_load, "slab", split_axis=2, concat_axis=1, tiled=True)
    xz_pred = jnp.transpose(xz_back, (0, 2, 3, 1))
    yz_pred = jnp.transpose(yz_back, (0, 2, 1, 3))
    merged_pred = (
        merging[0][:, None, None, None] * xy_pred
        + merging[1][:, None, None, None] * xz_pred
        + merging[2][:, None, None, None] * yz_pred
    )
    padded = with_halo(merged_pred, (("slab", 1),), 1)
    under_rim = jnp.where(position == 0, merged_pred[:, :1], padded[:, :1])
    over_rim = jnp.where(position == slab_count - 1, merged_pred[:, -1:], padded[:, -1:])
    lower_side = jnp.concatenate([under_rim, merged_pred[:, :-1]], axis=1)
    upper_side = jnp.concatenate([merged_pred[:, 1:], over_rim], axis=1)
    return median_three(lower_side, merged_pred, upper_side)


MESH = pl.DeviceIdType.MESH
f32 = jnp.float32
bf16 = jnp.bfloat16
REACH = 3


def split(x):
    hi = x.astype(bf16)
    return hi, (x - hi.astype(f32)).astype(bf16)


def mm(a, b):
    return lax.dot_general(a, b, (((1,), (0,)), ((), ())), preferred_element_type=f32)


def mm_nt(a, b):
    return lax.dot_general(a, b, (((1,), (1,)), ((), ())), preferred_element_type=f32)


def exact_mm(a, b):
    return lax.dot_general(
        a, b, (((1,), (0,)), ((), ())), preferred_element_type=f32, precision=exact_prec
    )


def product(mul, a, b):
    (a_hi, a_lo), (b_hi, b_lo) = a, b
    if mul is mm:
        return mul(
            jnp.concatenate([a_hi, a_lo, a_hi], axis=1),
            jnp.concatenate([b_hi, b_hi, b_lo], axis=0),
        )
    return mul(a_hi, b_hi) + (mul(a_hi, b_lo) + mul(a_lo, b_hi))


def iota(shape, dim):
    return lax.broadcasted_iota(jnp.int32, shape, dim)


def halo_plan(cz):
    plan = []
    left = REACH
    distance = 1
    while left > 0:
        count = min(cz, left)
        plan.append((distance, count))
        left -= count
        distance += 1
    return plan


def brick_kernel(
    slabs,
    vol_hbm,
    w1_hbm,
    b1_hbm,
    w2_hbm,
    b2_hbm,
    hw_hbm,
    hb_hbm,
    mg_hbm,
    out_ref,
    vbuf,
    w1_ref,
    b1_ref,
    w2_ref,
    b2_ref,
    hw_ref,
    hb_ref,
    mg_ref,
    pad_ref,
    send_sem,
    recv_sem,
    load_sem,
):
    cz, nx, ny = vol_hbm.shape
    ch = w1_ref.shape[0]
    heads = hw_ref.shape[0]
    lanes = ny * ch
    zi, zf, zo = cz + 6, cz + 4, cz + 2
    pos = lax.axis_index("slab")
    plan = halo_plan(cz)

    rim = jnp.zeros((REACH, nx, ny), f32)
    vbuf[:REACH] = rim
    vbuf[REACH + cz :] = rim

    sends = []
    for distance, count in plan[::-1]:
        sends.append((-distance, 0, count, REACH + distance * cz))
        sends.append((distance, cz - count, count, REACH - (distance - 1) * cz - count))

    def inside(index):
        return jnp.logical_and(index >= 0, index < slabs)

    loads = [
        pltpu.make_async_copy(source, target, load_sem.at[at])
        for at, (source, target) in enumerate(
            [
                (vol_hbm, vbuf.at[pl.ds(REACH, cz)]),
                (w2_hbm, w2_ref),
                (w1_hbm, w1_ref),
                (b1_hbm, b1_ref),
                (b2_hbm, b2_ref),
                (hw_hbm, hw_ref),
                (hb_hbm, hb_ref),
                (mg_hbm, mg_ref),
            ]
        )
    ]
    loads[0].start()
    barrier = pltpu.get_barrier_semaphore()
    expected = jnp.int32(0)
    for offset, _, _, _ in sends:
        there = inside(pos + offset)
        expected = expected + there.astype(jnp.int32)

        @pl.when(there)
        def _():
            pl.semaphore_signal(
                barrier, inc=1, device_id={"slab": pos + offset}, device_id_type=MESH
            )

    for load in loads[1:]:
        load.start()
    loads[0].wait()
    pl.semaphore_wait(barrier, expected)

    def copy_of(at):
        offset, first, count, slot = sends[at]
        return pltpu.make_async_remote_copy(
            src_ref=vbuf.at[pl.ds(REACH + first, count)],
            dst_ref=vbuf.at[pl.ds(slot, count)],
            send_sem=send_sem.at[at],
            recv_sem=recv_sem.at[at],
            device_id={"slab": pos + offset},
            device_id_type=MESH,
        )

    for at, (offset, _, _, _) in enumerate(sends):

        @pl.when(inside(pos + offset))
        def _():
            copy_of(at).start()

    for load in loads[1:]:
        load.wait()

    spread = (jnp.bitwise_and(iota((ch, lanes), 1), ch - 1) == iota((ch, lanes), 0)).astype(f32)
    b1 = exact_mm(b1_ref[...].reshape(1, ch), spread)
    b2 = exact_mm(b2_ref[...].reshape(1, ch), spread)
    w1_rows = exact_mm(w1_ref[...].T, spread)
    out_col = iota((ch, lanes), 1) // ch
    in_col = iota((ny, lanes), 0)
    col_gap = in_col - iota((ny, lanes), 1) // ch + 1
    first_parts = []
    for a in range(3):
        part = jnp.zeros((ny, lanes), f32)
        for b in range(3):
            row = w1_rows[3 * a + b : 3 * a + b + 1]
            part = jnp.where(col_gap == b, row, part)
        first_parts.append(part)
    first_w = split(jnp.concatenate(first_parts, axis=0))

    w2_t = w2_ref[...].reshape(9 * ch, ch).T
    spread_b = spread.astype(bf16)
    second_w = []
    for a in range(3):
        tiles = []
        for b in range(3):
            tap = 3 * a + b
            tiles.append([mm(v, spread_b) for v in split(w2_t[:, tap * ch : (tap + 1) * ch])])
        halves = []
        for half in range(2):
            rows = []
            for col in range(ny):
                block = jnp.where(out_col == col + 1, tiles[0][half], 0.0)
                block = jnp.where(out_col == col, tiles[1][half], block)
                block = jnp.where(out_col == col - 1, tiles[2][half], block)
                rows.append(block)
            halves.append(jnp.concatenate(rows, axis=0).astype(bf16))
        second_w.append(tuple(halves))

    hw_rows = exact_mm(hw_ref[...], spread)
    same = iota((ny, lanes), 0) == iota((ny, lanes), 1) // ch
    head_w = split(
        jnp.concatenate(
            [jnp.where(same, hw_rows[k : k + 1], 0.0) for k in range(heads)], axis=0
        )
    )

    for at, (offset, _, _, _) in enumerate(sends):

        @pl.when(inside(pos - offset))
        def _():
            copy_of(at).wait_recv()

    vol = vbuf[...].reshape(zi * nx, ny)
    vol_t = vol.T
    taps_yz = jnp.concatenate([vol[a * nx : (a + zf) * nx] for a in range(3)], axis=1)
    taps_xz = jnp.concatenate([vol_t[:, j * nx : (j + 3) * nx] for j in range(zf)], axis=0)
    row_x = jnp.bitwise_and(iota((zo * nx, ny), 0), nx - 1)
    mid = vol[2 * nx : (2 + zo) * nx]
    above = jnp.where(row_x == 0, 0.0, vol[2 * nx - 1 : (2 + zo) * nx - 1])
    below = jnp.where(row_x == nx - 1, 0.0, vol[2 * nx + 1 : (2 + zo) * nx + 1])
    taps_xy = jnp.concatenate([above, mid, below], axis=1)
    taps = split(jnp.concatenate([taps_xy, taps_xz, taps_yz], axis=0))
    hidden = jnp.maximum(product(mm, taps, first_w) + b1, 0.0)

    at_xz, at_yz, at_end = zo * nx, zo * nx + zf * ny, zo * nx + zf * ny + zf * nx
    slice_of = iota((zf * nx, lanes), 0) // nx + (pos * cz - 2)
    valid = jnp.logical_and(slice_of >= 0, slice_of < slabs * cz)
    hid_xz = split(jnp.where(valid, hidden[at_xz:at_yz], 0.0))
    hid_yz = split(jnp.where(valid, hidden[at_yz:at_end], 0.0))

    pad_ref[:, 0:8] = jnp.zeros((zo, 8, lanes), f32)
    pad_ref[:, nx + 8 : nx + 16] = jnp.zeros((zo, 8, lanes), f32)
    pad_ref[:, 8 : nx + 8] = hidden[:at_xz].reshape(zo, nx, lanes)

    summed = b2
    for a in range(3):
        hid_xy = split(pad_ref[:, 7 + a : 7 + a + nx].reshape(zo * nx, lanes))
        rows = tuple(
            jnp.concatenate(
                [
                    hid_xy[half],
                    hid_xz[half][a * ny : (a + zo) * ny],
                    hid_yz[half][a * nx : (a + zo) * nx],
                ],
                axis=0,
            )
            for half in range(2)
        )
        summed = summed + product(mm, rows, second_w[a])
    feats = split(jnp.maximum(summed, 0.0))
    f_xy, f_xz, f_yz = (
        tuple(v[j * zo * nx : (j + 1) * zo * nx] for v in feats) for j in range(3)
    )

    p_xy = product(mm_nt, f_xy, head_w)
    p_yz = product(mm_nt, f_yz, head_w)
    p_xz = product(mm_nt, head_w, f_xz)
    for k in range(heads):
        bias = hb_ref[k]
        w_xy, w_xz, w_yz = mg_ref[0, k], mg_ref[1, k], mg_ref[2, k]
        cols = slice(k * ny, (k + 1) * ny)
        merged = []
        flat = w_xy * (p_xy[:, cols] + bias) + w_yz * (p_yz[:, cols] + bias)
        side = w_xz * (p_xz[cols] + bias)
        for z in range(zo):
            merged.append(flat[z * nx : (z + 1) * nx] + side[:, z * ny : (z + 1) * ny])
        merged[0] = jnp.where(pos == 0, merged[1], merged[0])
        merged[-1] = jnp.where(pos == slabs - 1, merged[-2], merged[-1])
        for z in range(cz):
            out_ref[k, z] = median_three(merged[z], merged[z + 1], merged[z + 2])

    for at, (offset, _, _, _) in enumerate(sends):

        @pl.when(inside(pos + offset))
        def _():
            copy_of(at).wait_send()


def on_device_small(volume, *params):
    cz, nx, ny = volume.shape
    ch = params[0].shape[0]
    heads = params[4].shape[0]
    slabs = lax.axis_size("slab")
    copies = 2 * len(halo_plan(cz))
    return pl.pallas_call(
        lambda *refs: brick_kernel(slabs, *refs),
        out_shape=pltpu.VMEM((heads, cz, nx, ny), f32),
        in_specs=[pl.BlockSpec(memory_space=pltpu.HBM)] * 8,
        out_specs=pl.BlockSpec(memory_space=pltpu.VMEM),
        scratch_shapes=[
            pltpu.VMEM((cz + 2 * REACH, nx, ny), f32),
            *[pltpu.VMEM(param.shape, f32) for param in params[:5]],
            *[pltpu.SMEM(param.shape, f32) for param in params[5:]],
            pltpu.VMEM((cz + 2, nx + 16, ny * ch), f32),
            pltpu.SemaphoreType.DMA((copies,)),
            pltpu.SemaphoreType.DMA((copies,)),
            pltpu.SemaphoreType.DMA((8,)),
        ],
        compiler_params=pltpu.CompilerParams(
            collective_id=0, has_side_effects=True
        ),
        name="brick",
    )(volume, *params)


def on_device_any(volume, *params):
    _, nx, ny = volume.shape
    ch = params[0].shape[0]
    if nx == ny and nx % 16 == 0 and ch % 16 == 0 and nx & (nx - 1) == 0 and ch & (ch - 1) == 0:
        if ny * ch <= 512:
            return on_device_small(volume, *params)
    return on_device(volume, *params)


def solution(mesh):
    in_specs = (P(("groups", "slab"), None, None), P(), P(), P(), P(), P(), P(), P())
    out_specs = P(None, ("groups", "slab"), None, None)
    return jax.shard_map(
        on_device_any, mesh=mesh, in_specs=in_specs, out_specs=out_specs, check_vma=False
    )
```
